1024 devices in a mesh: expert: 16 (over x, core), shard: 64 (over z, y).
Axes of the slice: x: 8, y: 8, z: 8, core: 2. Of those that a mesh axis runs over, the one named last changes fastest.
Arguments:
- tokens: bfloat16 [1536, 2080], P('shard', 'expert'), may hold values from -6 to 6
- out_grad: bfloat16 [1536, 2080], P('shard', 'expert'), may hold values from -6 to 6
- gate_probs: bfloat16 [1536], P('shard'), may hold values from 0.19921875 to 1
- expert_ids: int32 [1536], P('shard'), may hold values from 0 to 15
- slots: int32 [1536], P('shard'), may hold values from -1 to 2, as said below
- w_in: bfloat16 [16, 2080, 6144], P('expert', None, 'shard'), may hold values from -0.125 to 0.125
- w_out: bfloat16 [16, 6144, 2080], P('expert', 'shard'), may hold values from -0.078125 to 0.078125
Outputs:
- token_grad: bfloat16 [1536, 2080], P('shard', 'expert')
- w_in_grad: float32 [16, 2080, 6144], P('expert', None, 'shard')
- w_out_grad: float32 [16, 6144, 2080], P('expert', 'shard')
The draws below stay inside these ranges and needn't reach their ends.
Inputs may be any that keep to these rules, and one draw needn't show every extreme that they name: `slots`: the token's place, counted from 0 in token order, among the tokens of its block of 24 that chose the same expert; -1 where that place is 3 or more (a dropped token).
All inputs are finite; a program needn't handle non-finite values.
Results may differ from the reference program's by a relative error of at most 0.0031.
Values may be sent and summed in bfloat16 or wider, within the bound.
A program may use at most 32 MiB of HBM per device.

```python
import jax
import jax.numpy as jnp
from jax import lax

D = 2080
FF = 6144
TOK_COL = 24
CAP = 3
EXPERTS = 16
TOKENS = 1536
N_SHARD = 64


def shared_routes(key):
    columns = TOKENS // TOK_COL
    key_base, key_hot, key_order = jax.random.split(key, 3)
    base_ids = jax.random.randint(key_base, (columns, TOK_COL), 0, EXPERTS)
    hot_ids = jax.random.randint(key_hot, (columns, 1), 0, EXPERTS)
    order_keys = jax.random.split(key_order, columns)

    def shuffle_one(one_key):
        return jax.random.permutation(one_key, TOK_COL)
    shuffled = jax.vmap(shuffle_one)(order_keys)
    forced = shuffled < CAP + CAP // 2 + 1
    chosen = jnp.where(forced, hot_ids, base_ids).astype(jnp.int32)
    one_hot = (chosen[:, :, None] == jnp.arange(EXPERTS, dtype=jnp.int32)[None, None, :]).astype(jnp.int32)
    earlier = jnp.cumsum(one_hot, axis=1) - one_hot
    placing = jnp.sum(earlier * one_hot, axis=2)
    kept_slot = jnp.where(placing < CAP, placing, -1).astype(jnp.int32)
    return (chosen.reshape(-1), kept_slot.reshape(-1))


def draw_expert_ids(key, part):
    return shared_routes(key)[0]


def draw_slots(key, part):
    return shared_routes(key)[1]


def shard_levels(stream_key, shape, pieces, low, top_value):
    loudness = 1.0
    for position, blocks in pieces:
        heights = jax.random.uniform(jax.random.fold_in(jax.random.fold_in(stream_key, 6), position), (blocks,), jnp.float32, low / len(pieces), top_value / len(pieces))
        loudness = loudness * jnp.repeat(jnp.exp(heights), shape[position] // blocks).reshape((-1,) + (1,) * (len(shape) - 1 - position))
    return loudness


def bell_draw(key, extent, deviation, limit, cuts=(), kind=jnp.bfloat16):
    result = deviation * jax.random.normal(key, extent, jnp.float32)
    if cuts:
        result = result * shard_levels(key, extent, cuts, -0.22, 0.18)
    return jnp.clip(result, -limit, limit).astype(kind)


def setup_inputs(seed: int = 0) -> dict:
    arg_keys = jax.random.split(jax.random.key(seed), 8)
    return {
        "tokens": bell_draw(arg_keys[0], (TOKENS, D), 1.0, 6.0, ((0, 64), (1, 16))),
        "out_grad": bell_draw(arg_keys[1], (TOKENS, D), 1.0, 6.0, ((0, 64), (1, 16))),
        "gate_probs": jnp.clip(0.19921875 + 0.80078125 * jax.random.uniform(arg_keys[2], (TOKENS,), jnp.float32) ** shard_levels(arg_keys[2], (TOKENS,), ((0, 64),), -0.2, 0.2), 0.19921875, 1.0).astype(jnp.bfloat16),
        "expert_ids": draw_expert_ids(jax.random.fold_in(arg_keys[7], 71), 0),
        "slots": draw_slots(jax.random.fold_in(arg_keys[7], 71), 0),
        "w_in": bell_draw(arg_keys[5], (EXPERTS, D, FF), D ** -0.5, 0.125, ((0, 16), (2, 64))),
        "w_out": bell_draw(arg_keys[6], (EXPERTS, FF, D), FF ** -0.5, 0.078125, ((0, 16), (1, 64))),
    }


root_two_over_pi = 0.7978845608028654
cubic_coef = 0.044715


def gelu_parts(pre_act):
    inner = root_two_over_pi * (pre_act + cubic_coef * pre_act * pre_act * pre_act)
    tanh_val = jnp.tanh(inner)
    value = 0.5 * pre_act * (1.0 + tanh_val)
    slope = 0.5 * (1.0 + tanh_val) + 0.5 * pre_act * (1.0 - tanh_val * tanh_val) * root_two_over_pi * (1.0 + 3.0 * cubic_coef * pre_act * pre_act)
    return value, slope


def expert_step(items):
    x_rows, g_rows, q_rows, w_first, w_second = items
    pre_act = jnp.dot(x_rows, w_first, preferred_element_type=jnp.float32)
    back_grad = jnp.dot(g_rows, w_second.T, preferred_element_type=jnp.float32)
    value, slope = gelu_parts(pre_act)
    gates = q_rows.astype(jnp.float32)[:, None]
    scaled = (gates * value).astype(jnp.bfloat16)
    dpre = (gates * back_grad * slope).astype(jnp.bfloat16)
    w_out_g = jnp.dot(scaled.T, g_rows, preferred_element_type=jnp.float32)
    w_in_g = jnp.dot(x_rows.T, dpre, preferred_element_type=jnp.float32)
    branch = jnp.dot(dpre, w_first.T, preferred_element_type=jnp.float32).astype(jnp.bfloat16)
    return branch, w_in_g, w_out_g


def reference(tokens, out_grad, gate_probs, expert_ids, slots, w_in, w_out):
    rows_total = N_SHARD * CAP
    column = (jnp.arange(TOKENS, dtype=jnp.int32) // TOK_COL).astype(jnp.int32)
    kept = slots >= 0
    dest = (column * CAP + jnp.maximum(slots, 0)).astype(jnp.int32)
    target = jnp.where(kept, expert_ids, EXPERTS).astype(jnp.int32)
    x_buf = jnp.zeros((EXPERTS, rows_total, D), jnp.bfloat16).at[target, dest].set(tokens, mode="drop")
    g_buf = jnp.zeros((EXPERTS, rows_total, D), jnp.bfloat16).at[target, dest].set(out_grad, mode="drop")
    q_buf = jnp.zeros((EXPERTS, rows_total), jnp.bfloat16).at[target, dest].set(gate_probs, mode="drop")
    branch_all, w_in_grad, w_out_grad = lax.map(expert_step, (x_buf, g_buf, q_buf, w_in, w_out))
    picked = branch_all[jnp.minimum(target, EXPERTS - 1), dest].astype(jnp.float32)
    total = out_grad.astype(jnp.float32) + jnp.where(kept[:, None], picked, jnp.zeros_like(picked))
    return total.astype(jnp.bfloat16), w_in_grad, w_out_grad
```

```python
import functools
import math

import jax
import jax.numpy as jnp
from jax import lax
from jax.experimental import pallas as pl
from jax.experimental.pallas import tpu as pltpu
from jax.sharding import PartitionSpec as P

CAP = 3
ROWS = 8
MESH = pl.DeviceIdType.MESH
f32 = jnp.float32
bf16 = jnp.bfloat16

root_two_over_pi = 0.7978845608028654
cubic_coef = 0.044715


def gelu_parts(pre_act):
    inner = root_two_over_pi * (pre_act + cubic_coef * pre_act * pre_act * pre_act)
    tanh_val = jnp.tanh(inner)
    value = 0.5 * pre_act * (1.0 + tanh_val)
    slope = 0.5 * (1.0 + tanh_val) + 0.5 * pre_act * (
        1.0 - tanh_val * tanh_val
    ) * root_two_over_pi * (1.0 + 3.0 * cubic_coef * pre_act * pre_act)
    return value, slope


def dot(left, right, contract):
    return lax.dot_general(left, right, ((contract[:1], contract[1:]), ((), ())), preferred_element_type=f32)


def remote(src, dst, send_sem, recv_sem, device):
    return pltpu.make_async_remote_copy(
        src_ref=src, dst_ref=dst, send_sem=send_sem, recv_sem=recv_sem, device_id=device, device_id_type=MESH
    )


class Exchange:
    def __init__(self, src_at, dst, sems, n, me, device_of):
        self.src_at, self.dst, self.sems, self.n, self.me, self.device_of = src_at, dst, sems, n, me, device_of

    def copy(self, d):
        other = lax.rem(self.me + d, self.n)
        return remote(
            self.src_at(other), self.dst.at[self.me], self.sems.at[0, d], self.sems.at[1, self.me], self.device_of(other)
        )

    def order(self):
        return sorted(range(1, self.n), key=lambda d: -min(d, self.n - d))

    def start(self):
        for d in self.order():
            self.copy(d).start()

    def wait_recv(self):
        for d in range(1, self.n):
            other = lax.rem(self.me + d, self.n)
            here = self.dst.at[other]
            remote(here, here, self.sems.at[0, d], self.sems.at[1, other], self.device_of(other)).wait_recv()

    def wait_send(self):
        for d in range(1, self.n):
            self.copy(d).wait_send()


class Chain:
    def __init__(self, blocks, sems, n, me, device_of, plus_parts):
        self.blocks, self.sems, self.n, self.me, self.device_of = blocks, sems, n, me, device_of
        self.parts = 3
        self.rows = blocks.shape[1] // self.parts
        self.plus_parts = plus_parts
        self.steps = n // 2
        self.waited = set()
        self.sent = []

    def block(self, index, part):
        return self.blocks.at[lax.rem(index + 2 * self.n, self.n), pl.ds(part * self.rows, self.rows)]

    def travels(self, way, step, part):
        if step < self.steps - 1:
            return True
        return (part in self.plus_parts) == (way == 0)

    def copy(self, way, step, part):
        sign = 1 if way == 0 else -1
        here = self.block(self.me - sign * step, part)
        device = self.device_of(lax.rem(self.me + sign + self.n, self.n))
        return remote(here, here, self.sems.at[0, way, step, part], self.sems.at[1, way, step, part], device)

    def receive(self, way, step, part):
        if (way, step, part) in self.waited or not self.travels(way, step, part):
            return
        self.waited.add((way, step, part))
        sign = 1 if way == 0 else -1
        here = self.block(self.me - sign * (step + 1), part)
        device = self.device_of(lax.rem(self.me + sign + self.n, self.n))
        remote(here, here, self.sems.at[0, way, step, part], self.sems.at[1, way, step, part], device).wait_recv()

    def send(self, way, step, part):
        if step > 0:
            self.receive(way, step - 1, part)
        if self.travels(way, step, part):
            copy = self.copy(way, step, part)
            copy.start()
            self.sent.append(copy)

    def finish(self):
        for step in range(self.steps):
            for part in range(self.parts):
                for way in (0, 1):
                    self.receive(way, step, part)

    def wait_send(self):
        for copy in self.sent:
            copy.wait_send()


def kernel(
    cfg, tok, og, gate, ids, slots, w1_hbm, w2_hbm,
    tok_out, g1_hbm, g2_hbm,
    w1, w2, wa, wb, w1b,
    send_a, recv_a, flat, gat_a, gat_b, rows_a, rows_b, perm,
    send_da, send_db, recv_da, recv_db, send_2a, send_2b, recv_2a, recv_2b,
    send_e, recv_e, grad1, grad2,
    sem_w, sem_g, sem_a, sem_b1, sem_b2, sem_d1, sem_d2, sem_e,
):
    ne, nz, ny, chunk, lanes_a, lanes_b = cfg
    features = ne * chunk
    half = features // 2
    hidden = w1.shape[0]
    e = lax.axis_index("expert")
    s = lax.axis_index("shard")
    z, y = s // ny, lax.rem(s, ny)

    def at_e(i):
        return (i, s)

    def at_z(i):
        return (e, i * ny + y)

    def at_y(i):
        return (e, z * ny + i)

    load1 = pltpu.make_async_copy(w1_hbm, w1, sem_w.at[0])
    load2 = pltpu.make_async_copy(w2_hbm, w2, sem_w.at[1])
    load1.start()
    load2.start()

    barrier = pltpu.get_barrier_semaphore()

    def greet(device):
        pl.semaphore_signal(barrier, inc=1, device_id=device, device_id_type=MESH)

    for d in range(1, ne):
        greet(at_e(lax.rem(e + d, ne)))
    for d in range(1, nz):
        greet(at_z(lax.rem(z + d, nz)))
    for d in range(1, ny):
        greet(at_y(lax.rem(y + d, ny)))
    in_a = e < ny
    last_shard = jnp.where(in_a, z * ny + e, (e - ny) * ny + y)
    for i in range(ne):
        @pl.when(jnp.logical_or(e != i, s != last_shard))
        def _():
            greet((jnp.int32(i), last_shard))
    own_a = e == y
    own_b = e == ny + z
    owned = jnp.where(jnp.logical_or(own_a, own_b), 1, 0)
    pl.semaphore_wait(barrier, (ne - 1) + (nz - 1) + (ny - 1) + nz + ny - owned)

    key = jnp.where(slots[...] >= 0, ids[...] * ROWS + slots[...], -100)
    row = lax.broadcasted_iota(jnp.int32, (ne * ROWS, tok.shape[0]), 0)
    pick_x = jnp.where(row == key, 1.0, 0.0).astype(bf16)
    pick_g = jnp.where(row == key + CAP, 1.0, 0.0).astype(bf16)
    sent = dot(pick_x, tok[...], (1, 0)) + dot(pick_g, og[...], (1, 0))
    send_a[...] = sent.reshape(ne, ROWS, chunk).astype(bf16)
    dispatch = Exchange(lambda i: send_a.at[i], recv_a, sem_a, ne, e, at_e)
    dispatch.start()
    recv_a[e] = send_a[e]

    row8 = lax.broadcasted_iota(jnp.int32, (ROWS, tok.shape[0]), 0) + e * ROWS
    gate_rows = jnp.sum(jnp.where(row8 == key, gate[...].astype(f32), 0.0), axis=1, keepdims=True)
    flat[:, features - features % 128:] = jnp.zeros((ROWS, flat.shape[1] - features + features % 128), f32)
    flat[:, features:features + 1] = gate_rows

    dispatch.wait_recv()
    for i in range(ne):
        flat[:, i * chunk:(i + 1) * chunk] = recv_a[i].astype(f32)
    gat_a[y] = flat[:, :lanes_a].astype(bf16)
    gat_b[z] = flat[:, lanes_a:].astype(bf16)

    first_a = Exchange(lambda i: gat_a.at[y], gat_a, sem_b1.at[0], ny, y, at_y)
    first_b = Exchange(lambda i: gat_b.at[z], gat_b, sem_b1.at[1], nz, z, at_z)
    first_a.start()
    first_b.start()

    load1.wait()
    load2.wait()
    wa[:hidden] = w1[:, :lanes_a]
    wa[hidden:] = w2[:, :lanes_a]
    rest = features - lanes_a
    wb[:, rest - rest % 128:] = jnp.zeros((2 * hidden, lanes_b - rest + rest % 128), bf16)
    wb[:hidden, :rest] = w1[:, lanes_a:]
    wb[hidden:, :rest] = w2[:, lanes_a:]
    w1b[...] = w1[:, half:]

    def dense(n):
        out = lax.broadcasted_iota(jnp.int32, (2 * CAP * n, n * ROWS), 0)
        src = lax.broadcasted_iota(jnp.int32, (2 * CAP * n, n * ROWS), 1)
        return jnp.where(src == lax.rem(out, n) * ROWS + out // n, 1.0, 0.0).astype(bf16)

    def packed(gat, n):
        return dot(dense(n), gat[...].reshape(n * ROWS, gat.shape[2]), (1, 0)).astype(bf16)

    chain_a = Chain(rows_a, sem_b2.at[0], nz, z, at_z, (0, 1))
    chain_b = Chain(rows_b, sem_b2.at[1], ny, y, at_y, (0,))
    first_a.wait_recv()
    rows_a[z] = packed(gat_a, ny)
    for part in range(3):
        for way in (0, 1):
            chain_a.send(way, 0, part)
    first_b.wait_recv()
    rows_b[y] = packed(gat_b, nz)
    for part in range(3):
        for way in (0, 1):
            chain_b.send(way, 0, part)
    for step in range(1, chain_a.steps):
        for part in range(3):
            for way in (0, 1):
                chain_a.send(way, step, part)
                chain_b.send(way, step, part)
    chain_a.finish()
    chain_b.finish()

    all_a = rows_a[...].reshape(nz * 2 * CAP * ny, lanes_a)
    all_b = rows_b[...].reshape(ny * 2 * CAP * nz, lanes_b)
    count = CAP * nz * ny
    lane = lax.broadcasted_iota(jnp.int32, (count, 2 * hidden), 1)

    def both(product, n, m):
        parts = product.reshape(n, 2, CAP * m, 2 * hidden)
        x_part = parts[:, 0].reshape(count, 2 * hidden)
        g_part = parts[:, 1].reshape(count, 2 * hidden)
        return jnp.where(lane < hidden, x_part, g_part)

    def reorder(value, n, m):
        for i in range(value.shape[1] // 128 + (value.shape[1] % 128 > 0)):
            perm[i, :, :min(128, value.shape[1] - 128 * i)] = value[:, 128 * i:128 * (i + 1)]
        pieces = []
        for j in range(m):
            for c in range(CAP):
                pieces.append(jnp.concatenate(
                    [perm[i, pl.ds(c * m + j, n, stride=CAP * m), :] for i in range(perm.shape[0])], axis=1))
        return jnp.concatenate(pieces, axis=0)[:, :value.shape[1]]

    hid_a = both(dot(all_a, wa[...], (1, 1)), nz, ny)
    hid_b = both(dot(all_b, wb[...], (1, 1)), ny, nz)
    hid = hid_b + reorder(hid_a, nz, ny)
    pre_act, back_grad = hid[:, :hidden], hid[:, hidden:]
    gate_lane = features - lanes_a
    gate_tile = gate_lane // 128 * 128
    gates = rows_b[:, :, gate_tile:gate_tile + 128].astype(f32)[:, :CAP * nz].reshape(count, 128)
    gates = gates[:, gate_lane - gate_tile:gate_lane - gate_tile + 1]
    value, slope = gelu_parts(pre_act)
    used_b = jnp.concatenate([gates * back_grad * slope, gates * value], axis=1)
    used_a = reorder(used_b, ny, nz)

    terms_a = dot(used_a[:, :hidden].astype(bf16), w1[:, :half], (1, 0))
    send_da[...] = terms_a.reshape(nz, CAP, ny, half).astype(bf16)
    sum_a = Exchange(lambda i: send_da.at[i], recv_da, sem_d1.at[0], nz, z, at_z)
    sum_a.start()
    recv_da[z] = send_da[z]
    terms_b = dot(used_b[:, :hidden].astype(bf16), w1b[...], (1, 0))
    send_db[...] = terms_b.reshape(ny, CAP, nz, half).astype(bf16)
    sum_b = Exchange(lambda i: send_db.at[i], recv_db, sem_d1.at[1], ny, y, at_y)
    sum_b.start()
    recv_db[y] = send_db[y]

    def spread(used, n, m):
        parts = used.reshape(n, 1, CAP * m, 2 * hidden)
        column = lax.broadcasted_iota(jnp.int32, parts.shape, 3)
        x_part = jnp.where(column < hidden, parts, 0.0)
        g_part = jnp.where(column < hidden, 0.0, parts)
        return jnp.concatenate([x_part, g_part], axis=1).reshape(n * 2 * CAP * m, 2 * hidden).astype(bf16)

    both_a = dot(spread(used_a, nz, ny), all_a, (0, 0))
    grad1[:, :lanes_a] = both_a[:hidden]
    grad2[:, :lanes_a] = both_a[hidden:]
    both_b = dot(spread(used_b, ny, nz), all_b, (0, 0))
    grad1[:, lanes_a:] = both_b[:hidden, :rest]
    grad2[:, lanes_a:] = both_b[hidden:, :rest]
    store1 = pltpu.make_async_copy(grad1, g1_hbm, sem_g.at[0])
    store2 = pltpu.make_async_copy(grad2, g2_hbm, sem_g.at[1])
    store1.start()
    store2.start()

    def second(first, recv, send, again, sems, n, m, me, device_of):
        first.wait_recv()
        total = recv[0].astype(f32)
        for i in range(1, n):
            total = total + recv[i].astype(f32)
        total = total.reshape(CAP * m, half)
        for j in range(m):
            send[j] = total[:, j * chunk:(j + 1) * chunk]
        exchange = Exchange(lambda i: send.at[i], again, sems, m, me, device_of)
        exchange.start()
        again[me] = send[me]
        return exchange

    again_a = second(sum_a, recv_da, send_2a, recv_2a, sem_d2.at[0], nz, ny, y, at_y)
    again_b = second(sum_b, recv_db, send_2b, recv_2b, sem_d2.at[1], ny, nz, z, at_z)

    def by_device(m):
        out = lax.broadcasted_iota(jnp.int32, (m * ROWS, CAP * m), 0)
        src = lax.broadcasted_iota(jnp.int32, (m * ROWS, CAP * m), 1)
        same = src == lax.rem(out, ROWS) * m + out // ROWS
        return jnp.where(jnp.logical_and(lax.rem(out, ROWS) < CAP, same), 1.0, 0.0).astype(bf16)

    def finish(exchange, again, m, send):
        exchange.wait_recv()
        total = again[0]
        for i in range(1, m):
            total = total + again[i]
        picked = dot(by_device(m), total.astype(bf16), (1, 0))
        send[...] = picked.reshape(m, ROWS, chunk).astype(bf16)

    finish(again_a, recv_2a, ny, send_e.at[0, :ny])

    def home(which, index, m, me, expert, shard_of, own):
        other = lax.rem(me + index, m)
        copy = remote(
            send_e.at[which, other], recv_e.at[e], sem_e.at[0, which * ny + index], sem_e.at[1, e],
            (expert, shard_of(other)),
        )
        if index > 0:
            return copy, None
        return copy, own

    homes = []
    for index in range(ny):
        homes.append(home(0, index, ny, y, y, lambda i: z * ny + i, own_a))

    def launch(copy, own, which, me):
        if own is None:
            copy.start()
        else:
            @pl.when(jnp.logical_not(own))
            def _():
                copy.start()

            @pl.when(own)
            def _():
                recv_e[e] = send_e[which, me]

    for copy, own in homes:
        launch(copy, own, 0, y)
    finish(again_b, recv_2b, nz, send_e.at[1, :nz])
    homes_b = []
    for index in range(nz):
        homes_b.append(home(1, index, nz, z, ny + z, lambda i: i * ny + y, own_b))
    for copy, own in homes_b:
        launch(copy, own, 1, z)

    for i in range(ne):
        here = recv_e.at[i]

        @pl.when(jnp.logical_or(e != i, s != last_shard))
        def _():
            remote(here, here, sem_e.at[0, 0], sem_e.at[1, i], (jnp.int32(i), last_shard)).wait_recv()

    branch = dot(pick_x, recv_e[...].reshape(ne * ROWS, chunk), (0, 0))
    tok_out[...] = (og[...].astype(f32) + branch).astype(bf16)

    for exchange in (dispatch, first_a, first_b, chain_a, chain_b, sum_a, sum_b, again_a, again_b):
        exchange.wait_send()
    for copy, own in homes + homes_b:
        if own is None:
            copy.wait_send()
        else:
            @pl.when(jnp.logical_not(own))
            def _():
                copy.wait_send()
    store1.wait()
    store2.wait()


def local(nz, ny, tokens, out_grad, gate_probs, expert_ids, slots, w_in, w_out):
    ne = lax.axis_size("expert")
    count, chunk = tokens.shape
    features = ne * chunk
    half = features // 2
    tiles = (features + 128) // 128
    lanes_a = 128 * ((tiles + 1) // 2)
    lanes_b = 128 * tiles - lanes_a
    w1 = jnp.swapaxes(w_in[0], 0, 1)
    w2 = w_out[0]
    hidden = w1.shape[0]
    cfg = (ne, nz, ny, chunk, lanes_a, lanes_b)
    vmem = pltpu.VMEM
    dma = pltpu.SemaphoreType.DMA
    most = max(nz, ny)
    scratch = [
        vmem((hidden, features), bf16),
        vmem((hidden, features), bf16),
        vmem((2 * hidden, lanes_a), bf16),
        vmem((2 * hidden, lanes_b), bf16),
        vmem((hidden, half), bf16),
        vmem((ne, ROWS, chunk), bf16),
        vmem((ne, ROWS, chunk), bf16),
        vmem((ROWS, lanes_a + lanes_b), f32),
        vmem((ny, ROWS, lanes_a), bf16),
        vmem((nz, ROWS, lanes_b), bf16),
        vmem((nz, 2 * CAP * ny, lanes_a), bf16),
        vmem((ny, 2 * CAP * nz, lanes_b), bf16),
        vmem((math.ceil(2 * hidden / 128), CAP * nz * ny, 128), f32),
        vmem((nz, CAP, ny, half), bf16),
        vmem((ny, CAP, nz, half), bf16),
        vmem((nz, CAP, ny, half), bf16),
        vmem((ny, CAP, nz, half), bf16),
        vmem((ny, CAP * ny, chunk), f32),
        vmem((nz, CAP * nz, chunk), f32),
        vmem((ny, CAP * ny, chunk), f32),
        vmem((nz, CAP * nz, chunk), f32),
        vmem((2, most, ROWS, chunk), bf16),
        vmem((ne, ROWS, chunk), bf16),
        vmem((hidden, features), f32),
        vmem((hidden, features), f32),
        dma((2,)),
        dma((2,)),
        dma((2, ne)),
        dma((2, 2, most)),
        dma((2, 2, 2, most // 2, 3)),
        dma((2, 2, most)),
        dma((2, 2, most)),
        dma((2, ne)),
    ]
    in_vmem = pl.BlockSpec(memory_space=pltpu.VMEM)
    anywhere = pl.BlockSpec(memory_space=pl.ANY)
    token_grad, g1, g2 = pl.pallas_call(
        functools.partial(kernel, cfg),
        out_shape=(
            jax.ShapeDtypeStruct((count, chunk), bf16),
            jax.ShapeDtypeStruct((hidden, features), f32),
            jax.ShapeDtypeStruct((hidden, features), f32),
        ),
        in_specs=[in_vmem] * 5 + [anywhere] * 2,
        out_specs=(in_vmem, anywhere, anywhere),
        scratch_shapes=scratch,
        compiler_params=pltpu.CompilerParams(
            collective_id=0, has_side_effects=True, vmem_limit_bytes=48 * 1024 * 1024
        ),
        name="moe_backward",
    )(tokens, out_grad, gate_probs[None], expert_ids[None], slots[None], w1, w2)
    return token_grad, jnp.swapaxes(g1, 0, 1)[None], g2[None]


def solution(mesh):
    placed = (
        P("shard", "expert"),
        P("shard", "expert"),
        P("shard"),
        P("shard"),
        P("shard"),
        P("expert", None, "shard"),
        P("expert", "shard", None),
    )
    ny = math.isqrt(mesh.shape["shard"])
    nz = mesh.shape["shard"] // ny
    return jax.shard_map(
        functools.partial(local, nz, ny),
        mesh=mesh,
        in_specs=placed,
        out_specs=(P("shard", "expert"), P("expert", None, "shard"), P("expert", "shard", None)),
        check_vma=False,
    )
```

```python
import functools
import math

import jax
import jax.numpy as jnp
from jax import lax
from jax.experimental import pallas as pl
from jax.experimental.pallas import tpu as pltpu
from jax.sharding import PartitionSpec as P

CAP = 3
ROWS = 8
MESH = pl.DeviceIdType.MESH
f32 = jnp.float32
bf16 = jnp.bfloat16

root_two_over_pi = 0.7978845608028654
cubic_coef = 0.044715


def gelu_parts(pre_act):
    inner = root_two_over_pi * (pre_act + cubic_coef * pre_act * pre_act * pre_act)
    tanh_val = jnp.tanh(inner)
    value = 0.5 * pre_act * (1.0 + tanh_val)
    slope = 0.5 * (1.0 + tanh_val) + 0.5 * pre_act * (
        1.0 - tanh_val * tanh_val
    ) * root_two_over_pi * (1.0 + 3.0 * cubic_coef * pre_act * pre_act)
    return value, slope


def dot(left, right, contract):
    return lax.dot_general(left, right, ((contract[:1], contract[1:]), ((), ())), preferred_element_type=f32)


def remote(src, dst, send_sem, recv_sem, device):
    return pltpu.make_async_remote_copy(
        src_ref=src, dst_ref=dst, send_sem=send_sem, recv_sem=recv_sem, device_id=device, device_id_type=MESH
    )


class Exchange:
    def __init__(self, src, dst, got, sems, n, me, device_of):
        self.src, self.dst, self.got, self.sems, self.n, self.me, self.device_of = src, dst, got, sems, n, me, device_of

    def copy(self, d):
        device = self.device_of(lax.rem(self.me + d, self.n))
        return remote(self.src(d), self.dst(d), self.sems.at[0, d], self.sems.at[1, d], device)

    def start(self, order):
        for d in order:
            self.copy(d).start()

    def wait_recv(self, order):
        for d in order:
            here = self.got(d)
            device = self.device_of(lax.rem(self.me + self.n - d, self.n))
            remote(here, here, self.sems.at[0, d], self.sems.at[1, d], device).wait_recv()

    def wait_send(self):
        for d in range(1, self.n):
            self.copy(d).wait_send()


def far_first(n):
    return sorted(range(1, n), key=lambda d: -min(d, n - d))


class Spread:
    def __init__(self, blocks, sems, n, me, device_of):
        self.blocks, self.sems, self.n, self.me, self.device_of = blocks, sems, n, me, device_of
        self.waited = set()
        self.sent = []
        if n > 4:
            self.first = {0: (-2, 2), 1: (2, -2), 2: (-1, 1), 3: (1, -1)}
            self.second = {4: (-3, 1), 5: (3, -1), 6: (4, 2), 7: (4, -2)}
        else:
            self.first = {0: (1, 1)}
            self.second = {}

    def block(self, distance, part):
        return self.blocks.at[(distance + self.n // 2 - 1) % self.n, part]

    def copy(self, index, part):
        distance, places = {**self.first, **self.second}[index]
        device = self.device_of(lax.rem(self.me + places + self.n, self.n))
        src, dst = self.block(distance + places, part), self.block(distance, part)
        return remote(src, dst, self.sems.at[0, index, part], self.sems.at[1, index, part], device)

    def send(self, index, part):
        copy = self.copy(index, part)
        copy.start()
        self.sent.append(copy)

    def receive(self, index, part):
        if (index, part) in self.waited:
            return
        self.waited.add((index, part))
        distance, places = {**self.first, **self.second}[index]
        device = self.device_of(lax.rem(self.me - places + self.n, self.n))
        here = self.block(distance, part)
        remote(here, here, self.sems.at[0, index, part], self.sems.at[1, index, part], device).wait_recv()

    def start(self, part):
        for index in self.first:
            self.send(index, part)

    def forward(self, part):
        if self.second:
            for index, through, across in ((0, 4, 6), (1, 5, 7)):
                self.receive(index, part)
                if part == index:
                    self.send(across, part)
                self.send(through, part)

    def finish(self, part):
        for index in self.first:
            self.receive(index, part)
        if self.second:
            for index in (4, 5, 6 + part):
                self.receive(index, part)

    def wait_send(self):
        for copy in self.sent:
            copy.wait_send()


def kernel(
    cfg, tok_hbm, og_hbm, gate_hbm, ids_hbm, slots_hbm, w1_hbm, w2_hbm,
    tok_out, grad1, grad2,
    tok, og, gate, ids, slots, w1, w2, wa, wb, w1b,
    send_a, recv_a, flat, gat_a, gat_b, rows_a, rows_b, hid_a, hid_b, used, used_a, used_b,
    send_da, send_db, recv_da, recv_db, fold, send_2a, send_2b, recv_2a, recv_2b,
    send_e, recv_e,
    sem_w, sem_a, sem_b1, sem_b2, sem_d1, sem_d2, sem_e,
):
    ne, nz, ny, chunk, lanes_a, lanes_b = cfg
    n = nz
    features = ne * chunk
    half = features // 2
    rest = features - lanes_a
    hidden = w1.shape[0]
    per = 2 * CAP
    block_rows = n * per
    count = CAP * n * n
    e = lax.axis_index("expert")
    s = lax.axis_index("shard")
    z, y = s // ny, lax.rem(s, ny)

    def at_e(i):
        return (i, s)

    def at_z(i):
        return (e, i * ny + y)

    def at_y(i):
        return (e, z * ny + i)

    barrier = pltpu.get_barrier_semaphore()
    for device_of, me, size in ((at_e, e, ne), (at_z, z, nz), (at_y, y, ny)):
        for d in far_first(size):
            pl.semaphore_signal(barrier, inc=1, device_id=device_of(lax.rem(me + d, size)), device_id_type=MESH)

    sources = (tok_hbm, og_hbm, gate_hbm, ids_hbm, slots_hbm, w1_hbm, w2_hbm)
    places = (tok, og, gate, ids, slots, w1, w2)
    loads = [pltpu.make_async_copy(src, dst, sem_w.at[i]) for i, (src, dst) in enumerate(zip(sources, places))]
    for load in loads:
        load.start()

    for load in loads[:5]:
        load.wait()
    key = jnp.where(slots[...] >= 0, ids[...] * ROWS + slots[...], -100)
    row = lax.broadcasted_iota(jnp.int32, (ne * ROWS, tok.shape[0]), 0)
    pick_x = jnp.where(row == key, 1.0, 0.0).astype(bf16)
    pick_g = jnp.where(row == key + CAP, 1.0, 0.0).astype(bf16)
    sent = dot(pick_x, tok[...], (1, 0)) + dot(pick_g, og[...], (1, 0))
    send_a[...] = sent.reshape(ne, ROWS, chunk).astype(bf16)
    row8 = lax.broadcasted_iota(jnp.int32, (ROWS, tok.shape[0]), 0) + e * ROWS
    gate_rows = jnp.sum(jnp.where(row8 == key, gate[...].astype(f32), 0.0), axis=1, keepdims=True)
    flat[:, features - features % 128:] = jnp.zeros((ROWS, flat.shape[1] - features + features % 128), f32)
    flat[:, features:features + 1] = gate_rows

    pl.semaphore_wait(barrier, (ne - 1) + (nz - 1) + (ny - 1))

    dispatch = Exchange(
        lambda d: send_a.at[lax.rem(e + d, ne)], lambda d: recv_a.at[e], lambda d: recv_a.at[lax.rem(e + ne - d, ne)],
        sem_a, ne, e, at_e)
    dispatch.start(far_first(ne))
    recv_a[e] = send_a[e]

    loads[5].wait()
    loads[6].wait()
    wa[...] = jnp.zeros(wa.shape, bf16)
    wb[...] = jnp.zeros(wb.shape, bf16)
    wa[:hidden] = w1[:, :lanes_a]
    wa[128:128 + hidden] = w2[:, :lanes_a]
    wb[:hidden, :rest] = w1[:, lanes_a:]
    wb[128:128 + hidden, :rest] = w2[:, lanes_a:]
    gate_unit = lax.broadcasted_iota(jnp.int32, (16, lanes_b), 0) == 0
    gate_lane = lax.broadcasted_iota(jnp.int32, (16, lanes_b), 1) == rest
    wb[hidden:hidden + 16] = jnp.where(jnp.logical_and(gate_unit, gate_lane), 1.0, 0.0).astype(bf16)
    w1b[...] = w1[:, half:]
    used_a[...] = jnp.zeros(used_a.shape, f32)
    used_b[...] = jnp.zeros(used_b.shape, f32)
    send_2a[...] = jnp.zeros(send_2a.shape, f32)
    send_2b[...] = jnp.zeros(send_2b.shape, f32)

    dispatch.wait_recv(range(1, ne))
    for i in range(ne):
        flat[:, i * chunk:(i + 1) * chunk] = recv_a[i].astype(f32)

    def place(distance):
        return (distance + 1) % n

    def first(gat, sems, me, device_of):
        mine = place(0)
        return Exchange(lambda d: gat.at[mine], lambda d: gat.at[place(-d)], lambda d: gat.at[place(-d)], sems, n, me, device_of)

    near = [d for d in range(1, n) if place(-d) < n // 2]
    far = [d for d in range(1, n) if place(-d) >= n // 2]
    first_a = first(gat_a, sem_b1.at[0], y, at_y)
    first_b = first(gat_b, sem_b1.at[1], z, at_z)
    gat_a[place(0)] = flat[:, :lanes_a].astype(bf16)
    first_a.start(near + far)
    gat_b[place(0)] = flat[:, lanes_a:].astype(bf16)
    first_b.start(near + far)

    out = lax.broadcasted_iota(jnp.int32, (block_rows // 2, n // 2 * ROWS), 0)
    src = lax.broadcasted_iota(jnp.int32, (block_rows // 2, n // 2 * ROWS), 1)
    dense = jnp.where(src == out // per * ROWS + lax.rem(out, per), 1.0, 0.0).astype(bf16)

    def packed(gat, part):
        piece = gat[part * (n // 2):(part + 1) * (n // 2)]
        return dot(dense, piece.reshape(n // 2 * ROWS, gat.shape[2]), (1, 0))

    spread_a = Spread(rows_a, sem_b2.at[0], nz, z, at_z)
    spread_b = Spread(rows_b, sem_b2.at[1], ny, y, at_y)
    for part, group in ((0, near), (1, far)):
        for exchange, spread, gat in ((first_a, spread_a, gat_a), (first_b, spread_b, gat_b)):
            exchange.wait_recv(group)
            blocks = spread.blocks
            blocks[n // 2 - 1, part] = packed(gat, part).reshape(blocks.shape[2:]).astype(bf16)
            spread.start(part)
    for part in (0, 1):
        for spread in (spread_a, spread_b):
            spread.forward(part)
    for part in (0, 1):
        for spread in (spread_a, spread_b):
            spread.finish(part)

    def block_of(i):
        return (i - 1 + n // 2 - 1) % n

    all_a = rows_a[...].reshape(n * block_rows, lanes_a)
    all_b = rows_b[...].reshape(n * block_rows, lanes_b)
    for hid, rows, weights in ((hid_a, all_a, wa), (hid_b, all_b, wb)):
        product = dot(rows, weights[...], (1, 1))
        for i in range(n):
            here = product[block_of(i) * block_rows:(block_of(i) + 1) * block_rows]
            hid[0, i * block_rows:(i + 1) * block_rows] = here[:, :128]
            hid[1, i * block_rows:(i + 1) * block_rows] = here[:, 128:]

    def gathered(which, q):
        return jnp.concatenate([
            hid_a[which, pl.ds(i * block_rows + q, n, stride=per), :]
            + hid_b[which, pl.ds(i * per + q, n, stride=block_rows), :] for i in range(n)], axis=0)

    for c in range(CAP):
        pre_act = gathered(0, c)
        back_grad = gathered(1, CAP + c)
        gates = pre_act[:, hidden:hidden + 1]
        value, slope = gelu_parts(pre_act)
        used[0, c * n * n:(c + 1) * n * n] = gates * back_grad * slope
        used[1, c * n * n:(c + 1) * n * n] = gates * value

    def terms(rows, weights, send):
        result = dot(rows[:, :hidden].astype(bf16), weights, (1, 0))
        send[...] = result.reshape(send.shape).astype(bf16)

    def first_sum(send, recv, sems, me, device_of):
        return Exchange(lambda d: send.at[place(d)], lambda d: recv.at[d], lambda d: recv.at[d], sems, n, me, device_of)

    order_a = [used[0, (c * n + i) * n:(c * n + i + 1) * n, :] for i in range(n) for c in range(CAP)]
    terms(jnp.concatenate(order_a, axis=0), w1[:, :half], send_da)
    sum_a = first_sum(send_da, recv_da, sem_d1.at[0], z, at_z)
    sum_a.start(far_first(n))
    order_b = [used[0, pl.ds(c * n * n + i, n, stride=n), :] for i in range(n) for c in range(CAP)]
    terms(jnp.concatenate(order_b, axis=0), w1b[...], send_db)
    sum_b = first_sum(send_db, recv_db, sem_d1.at[1], y, at_y)
    sum_b.start(far_first(n))

    for c in range(CAP):
        for i in range(n):
            for which in (0, 1):
                q = which * CAP + c
                piece = used[which, (c * n + i) * n:(c * n + i + 1) * n, :]
                used_a[which, pl.ds(block_of(i) * block_rows + q, n, stride=per), :] = piece
    for c in range(CAP):
        for i in range(n):
            for which in (0, 1):
                q = which * CAP + c
                piece = used[which, pl.ds(c * n * n + i, n, stride=n), :]
                used_b[which, pl.ds(block_of(i) * block_rows + q, n, stride=per), :] = piece

    for pieces, rows, first_lane, width in ((used_a, all_a, 0, lanes_a), (used_b, all_b, lanes_a, rest)):
        both = jnp.concatenate([pieces[0], pieces[1]], axis=1).astype(bf16)
        product = dot(both, rows, (0, 0))
        grad1[:, first_lane:first_lane + width] = product[:hidden, :width]
        grad2[:, first_lane:first_lane + width] = product[128:128 + hidden, :width]

    quarter = half // 2
    tiles = fold.shape[0]

    def second(exchange, send_first, recv, send, again, sems, me, device_of):
        exchange.wait_recv(far_first(n)[::-1])
        total = send_first[place(0)].astype(f32)
        for d in range(1, n):
            total = total + recv[d].astype(f32)
        total = total.reshape(CAP * n, half)
        for h in (0, 1):
            piece = total[:, h * quarter:(h + 1) * quarter]
            for t in range(tiles):
                width = min(128, quarter - 128 * t)
                fold[t, h * CAP * n:(h + 1) * CAP * n, :width] = piece[:, 128 * t:128 * t + width]
        for i in range(n):
            for t in range(tiles):
                width = min(128, quarter - 128 * t)
                send[i, :per, 128 * t:128 * t + width] = fold[t, pl.ds(i, per, stride=n), :][:, :width]
        again_sum = Exchange(lambda d: send.at[place(d)], lambda d: again.at[d], lambda d: again.at[d], sems, n, me, device_of)
        again_sum.start(far_first(n))
        return again_sum

    again_a = second(sum_a, send_da, recv_da, send_2a, recv_2a, sem_d2.at[0], y, at_y)
    again_b = second(sum_b, send_db, recv_db, send_2b, recv_2b, sem_d2.at[1], z, at_z)

    quarter_chunks = ne // 4
    for which, exchange, send, again in ((0, again_a, send_2a, recv_2a), (1, again_b, send_2b, recv_2b)):
        exchange.wait_recv(far_first(n)[::-1])
        total = send[place(0)]
        for d in range(1, n):
            total = total + again[d]
        for i in range(quarter_chunks):
            send_e[which * quarter_chunks + i] = total[:, i * chunk:(i + 1) * chunk].astype(bf16)

    def block_for(i):
        return i // (ne // 2) * quarter_chunks + lax.rem(i, quarter_chunks)

    back = Exchange(
        lambda d: send_e.at[block_for(lax.rem(e + d, ne))], lambda d: recv_e.at[e], lambda d: recv_e.at[lax.rem(e + ne - d, ne)],
        sem_e, ne, e, at_e)
    back.start(far_first(ne))
    recv_e[e] = send_e[block_for(e)]
    my_quarter = lax.rem(e, ne // 2) // quarter_chunks
    pick_e = jnp.where(row == key + my_quarter * CAP, 1.0, 0.0).astype(bf16)
    for exchange in (dispatch, first_a, first_b, spread_a, spread_b, sum_a, sum_b, again_a, again_b):
        exchange.wait_send()
    back.wait_recv(range(1, ne))
    branch = dot(pick_e, recv_e[...].reshape(ne * ROWS, chunk), (0, 0))
    tok_out[...] = (og[...].astype(f32) + branch).astype(bf16)
    back.wait_send()


def local(nz, ny, tokens, out_grad, gate_probs, expert_ids, slots, w_in, w_out):
    ne = lax.axis_size("expert")
    n = nz
    tokens_here, chunk = tokens.shape
    features = ne * chunk
    half = features // 2
    tiles = (features + 128) // 128
    lanes_a = 128 * ((tiles + 1) // 2)
    lanes_b = 128 * tiles - lanes_a
    w1 = jnp.swapaxes(w_in[0], 0, 1)
    w2 = w_out[0]
    hidden = w1.shape[0]
    cfg = (ne, nz, ny, chunk, lanes_a, lanes_b)
    vmem = pltpu.VMEM
    dma = pltpu.SemaphoreType.DMA
    per = 2 * CAP
    part_rows = n * per // 2
    step_rows = math.gcd(8, part_rows)
    scratch = [
        vmem((tokens_here, chunk), bf16),
        vmem((tokens_here, chunk), bf16),
        vmem((1, tokens_here), bf16),
        vmem((1, tokens_here), jnp.int32),
        vmem((1, tokens_here), jnp.int32),
        vmem((hidden, features), bf16),
        vmem((hidden, features), bf16),
        vmem((256, lanes_a), bf16),
        vmem((256, lanes_b), bf16),
        vmem((hidden, half), bf16),
        vmem((ne, ROWS, chunk), bf16),
        vmem((ne, ROWS, chunk), bf16),
        vmem((ROWS, lanes_a + lanes_b), f32),
        vmem((n, ROWS, lanes_a), bf16),
        vmem((n, ROWS, lanes_b), bf16),
        vmem((n, 2, part_rows // step_rows, step_rows, lanes_a), bf16),
        vmem((n, 2, part_rows // step_rows, step_rows, lanes_b), bf16),
        vmem((2, n * n * per, 128), f32),
        vmem((2, n * n * per, 128), f32),
        vmem((2, CAP * n * n, 128), f32),
        vmem((2, n * n * per, 128), f32),
        vmem((2, n * n * per, 128), f32),
        vmem((n, CAP, n, half), bf16),
        vmem((n, CAP, n, half), bf16),
        vmem((n, CAP, n, half), bf16),
        vmem((n, CAP, n, half), bf16),
        vmem((math.ceil(half // 2 / 128), per * n, 128), f32),
        vmem((n, ROWS, half // 2), f32),
        vmem((n, ROWS, half // 2), f32),
        vmem((n, ROWS, half // 2), f32),
        vmem((n, ROWS, half // 2), f32),
        vmem((ne // 2, ROWS, chunk), bf16),
        vmem((ne, ROWS, chunk), bf16),
        dma((7,)),
        dma((2, ne)),
        dma((2, 2, n)),
        dma((2, 2, 8, 2)),
        dma((2, 2, n)),
        dma((2, 2, n)),
        dma((2, ne)),
    ]
    in_vmem = pl.BlockSpec(memory_space=pltpu.VMEM)
    in_hbm = pl.BlockSpec(memory_space=pltpu.HBM)
    operands = (tokens, out_grad, gate_probs[None], expert_ids[None], slots[None], w1, w2)
    token_grad, g1, g2 = pl.pallas_call(
        functools.partial(kernel, cfg),
        out_shape=(
            jax.ShapeDtypeStruct((tokens_here, chunk), bf16),
            jax.ShapeDtypeStruct((hidden, features), f32),
            jax.ShapeDtypeStruct((hidden, features), f32),
        ),
        in_specs=[in_hbm] * 7,
        out_specs=(in_vmem,) * 3,
        scratch_shapes=scratch,
        compiler_params=pltpu.CompilerParams(
            collective_id=0, has_side_effects=True, vmem_limit_bytes=48 * 1024 * 1024
        ),
        name="moe_backward",
    )(*[pltpu.with_memory_space_constraint(value, pltpu.HBM) for value in operands])
    return token_grad, jnp.swapaxes(g1, 0, 1)[None], g2[None]


def solution(mesh):
    placed = (
        P("shard", "expert"),
        P("shard", "expert"),
        P("shard"),
        P("shard"),
        P("shard"),
        P("expert", None, "shard"),
        P("expert", "shard", None),
    )
    ny = math.isqrt(mesh.shape["shard"])
    nz = mesh.shape["shard"] // ny
    return jax.shard_map(
        functools.partial(local, nz, ny),
        mesh=mesh,
        in_specs=placed,
        out_specs=(P("shard", "expert"), P("expert", None, "shard"), P("expert", "shard", None)),
        check_vma=False,
    )
```

```python
import functools
import math

import jax
import jax.numpy as jnp
from jax import lax
from jax.experimental import pallas as pl
from jax.experimental.pallas import tpu as pltpu
from jax.sharding import PartitionSpec as P

CAP = 3
ROWS = 8
MESH = pl.DeviceIdType.MESH
f32 = jnp.float32
bf16 = jnp.bfloat16

root_two_over_pi = 0.7978845608028654
cubic_coef = 0.044715


def gelu_parts(pre_act):
    inner = root_two_over_pi * (pre_act + cubic_coef * pre_act * pre_act * pre_act)
    tanh_val = jnp.tanh(inner)
    value = 0.5 * pre_act * (1.0 + tanh_val)
    slope = 0.5 * (1.0 + tanh_val) + 0.5 * pre_act * (
        1.0 - tanh_val * tanh_val
    ) * root_two_over_pi * (1.0 + 3.0 * cubic_coef * pre_act * pre_act)
    return value, slope


def dot(left, right, contract):
    return lax.dot_general(left, right, ((contract[:1], contract[1:]), ((), ())), preferred_element_type=f32)


def remote(src, dst, send_sem, recv_sem, device):
    return pltpu.make_async_remote_copy(
        src_ref=src, dst_ref=dst, send_sem=send_sem, recv_sem=recv_sem, device_id=device, device_id_type=MESH
    )


class Exchange:
    def __init__(self, src, dst, got, sems, n, me, device_of):
        self.src, self.dst, self.got, self.sems, self.n, self.me, self.device_of = src, dst, got, sems, n, me, device_of

    def copy(self, d):
        device = self.device_of(lax.rem(self.me + d, self.n))
        return remote(self.src(d), self.dst(d), self.sems.at[0, d], self.sems.at[1, d], device)

    def start(self, order):
        for d in order:
            self.copy(d).start()

    def wait_recv(self, order):
        for d in order:
            here = self.got(d)
            device = self.device_of(lax.rem(self.me + self.n - d, self.n))
            remote(here, here, self.sems.at[0, d], self.sems.at[1, d], device).wait_recv()

    def wait_send(self):
        for d in range(1, self.n):
            self.copy(d).wait_send()


def far_first(n):
    return sorted(range(1, n), key=lambda d: -min(d, n - d))


class Spread:
    def __init__(self, blocks, sems, n, me, device_of):
        self.blocks, self.sems, self.n, self.me, self.device_of = blocks, sems, n, me, device_of
        self.waited = set()
        self.sent = []
        if n > 4:
            self.first = {0: (-2, 2), 1: (2, -2), 2: (-1, 1), 3: (1, -1)}
            self.second = {4: (-3, 1), 5: (3, -1), 6: (4, 2), 7: (4, -2)}
        else:
            self.first = {0: (1, 1)}
            self.second = {}

    def block(self, distance, part):
        return self.blocks.at[(distance + self.n // 2 - 1) % self.n, part]

    def copy(self, index, part):
        distance, places = {**self.first, **self.second}[index]
        device = self.device_of(lax.rem(self.me + places + self.n, self.n))
        src, dst = self.block(distance + places, part), self.block(distance, part)
        return remote(src, dst, self.sems.at[0, index, part], self.sems.at[1, index, part], device)

    def send(self, index, part):
        copy = self.copy(index, part)
        copy.start()
        self.sent.append(copy)

    def receive(self, index, part):
        if (index, part) in self.waited:
            return
        self.waited.add((index, part))
        distance, places = {**self.first, **self.second}[index]
        device = self.device_of(lax.rem(self.me - places + self.n, self.n))
        here = self.block(distance, part)
        remote(here, here, self.sems.at[0, index, part], self.sems.at[1, index, part], device).wait_recv()

    def start(self, part):
        for index in self.first:
            self.send(index, part)

    def forward(self, part):
        if self.second:
            for index, through, across in ((0, 4, 6), (1, 5, 7)):
                self.receive(index, part)
                if part == index:
                    self.send(across, part)
                self.send(through, part)

    def finish(self, part):
        for index in self.first:
            self.receive(index, part)
        if self.second:
            for index in (4, 5, 6 + part):
                self.receive(index, part)

    def wait_send(self):
        for copy in self.sent:
            copy.wait_send()


def kernel(
    cfg, tok_hbm, og_hbm, gate_hbm, ids_hbm, slots_hbm, w1_hbm, w2_hbm,
    tok_out, grad1, grad2,
    tok, og, gate, ids, slots, w1, w2, wa, wb, w1b,
    send_a, recv_a, flat, gat_a, gat_b, rows_a, rows_b, hid_a, hid_b, used, used_a, used_b,
    send_da, send_db, recv_da, recv_db, send_2a, send_2b, recv_2a, recv_2b,
    send_e, recv_e,
    sem_w, sem_a, sem_b1, sem_b2, sem_d1, sem_d2, sem_e,
):
    ne, nz, ny, chunk, lanes_a, lanes_b = cfg
    n = nz
    features = ne * chunk
    half = features // 2
    rest = features - lanes_a
    hidden = w1.shape[0]
    per = 2 * CAP
    block_rows = n * per
    count = CAP * n * n
    e = lax.axis_index("expert")
    s = lax.axis_index("shard")
    z, y = s // ny, lax.rem(s, ny)

    def at_e(i):
        return (i, s)

    def at_z(i):
        return (e, i * ny + y)

    def at_y(i):
        return (e, z * ny + i)

    sources = (tok_hbm, og_hbm, gate_hbm, ids_hbm, slots_hbm, w1_hbm, w2_hbm)
    places = (tok, og, gate, ids, slots, w1, w2)
    loads = [pltpu.make_async_copy(src, dst, sem_w.at[i]) for i, (src, dst) in enumerate(zip(sources, places))]
    for load in loads:
        load.start()

    barrier = pltpu.get_barrier_semaphore()
    for device_of, me, size in ((at_e, e, ne), (at_z, z, nz), (at_y, y, ny)):
        for d in far_first(size):
            pl.semaphore_signal(barrier, inc=1, device_id=device_of(lax.rem(me + d, size)), device_id_type=MESH)

    for load in loads[:5]:
        load.wait()
    key = jnp.where(slots[...] >= 0, ids[...] * ROWS + slots[...], -100)
    row = lax.broadcasted_iota(jnp.int32, (ne * ROWS, tok.shape[0]), 0)
    pick_x = jnp.where(row == key, 1.0, 0.0).astype(bf16)
    pick_g = jnp.where(row == key + CAP, 1.0, 0.0).astype(bf16)
    sent = dot(pick_x, tok[...], (1, 0)) + dot(pick_g, og[...], (1, 0))
    send_a[...] = sent.reshape(ne, ROWS, chunk).astype(bf16)
    row8 = lax.broadcasted_iota(jnp.int32, (ROWS, tok.shape[0]), 0) + e * ROWS
    gate_rows = jnp.sum(jnp.where(row8 == key, gate[...].astype(f32), 0.0), axis=1, keepdims=True)
    flat[:, features - features % 128:] = jnp.zeros((ROWS, flat.shape[1] - features + features % 128), f32)
    flat[:, features:features + 1] = gate_rows

    pl.semaphore_wait(barrier, (ne - 1) + (nz - 1) + (ny - 1))

    dispatch = Exchange(
        lambda d: send_a.at[lax.rem(e + d, ne)], lambda d: recv_a.at[e], lambda d: recv_a.at[lax.rem(e + ne - d, ne)],
        sem_a, ne, e, at_e)
    dispatch.start(far_first(ne))
    recv_a[e] = send_a[e]

    loads[5].wait()
    loads[6].wait()
    wa[...] = jnp.zeros(wa.shape, bf16)
    wb[...] = jnp.zeros(wb.shape, bf16)
    wa[:hidden] = w1[:, :lanes_a]
    wa[128:128 + hidden] = w2[:, :lanes_a]
    wb[:hidden, :rest] = w1[:, lanes_a:]
    wb[128:128 + hidden, :rest] = w2[:, lanes_a:]
    gate_unit = lax.broadcasted_iota(jnp.int32, (16, lanes_b), 0) == 0
    gate_lane = lax.broadcasted_iota(jnp.int32, (16, lanes_b), 1) == rest
    wb[hidden:hidden + 16] = jnp.where(jnp.logical_and(gate_unit, gate_lane), 1.0, 0.0).astype(bf16)
    w1b[...] = w1[:, half:]
    used_a[...] = jnp.zeros(used_a.shape, f32)
    used_b[...] = jnp.zeros(used_b.shape, f32)
    send_2a[...] = jnp.zeros(send_2a.shape, f32)
    send_2b[...] = jnp.zeros(send_2b.shape, f32)

    dispatch.wait_recv(range(1, ne))
    for i in range(ne):
        flat[:, i * chunk:(i + 1) * chunk] = recv_a[i].astype(f32)
    for base, gat in ((0, gat_a), (lanes_a, gat_b)):
        for k in range(ROWS - per):
            tail = base + gat.shape[2] + 128 * k
            for q in range(per):
                flat[per + k:per + k + 1, base + 128 * q:base + 128 * (q + 1)] = flat[q:q + 1, tail:tail + 128]

    def place(distance):
        return (distance + 1) % n

    def first(gat, sems, me, device_of):
        mine = place(0)
        return Exchange(lambda d: gat.at[mine], lambda d: gat.at[place(-d)], lambda d: gat.at[place(-d)], sems, n, me, device_of)

    near = [d for d in range(1, n) if place(-d) < n // 2]
    far = [d for d in range(1, n) if place(-d) >= n // 2]
    first_a = first(gat_a, sem_b1.at[0], y, at_y)
    first_b = first(gat_b, sem_b1.at[1], z, at_z)
    gat_a[place(0)] = flat[:, :gat_a.shape[2]].astype(bf16)
    first_a.start(near + far)
    gat_b[place(0)] = flat[:, lanes_a:lanes_a + gat_b.shape[2]].astype(bf16)
    first_b.start(near + far)

    out = lax.broadcasted_iota(jnp.int32, (block_rows // 2, n // 2 * ROWS), 0)
    src = lax.broadcasted_iota(jnp.int32, (block_rows // 2, n // 2 * ROWS), 1)
    dense = jnp.where(src == out // per * ROWS + lax.rem(out, per), 1.0, 0.0).astype(bf16)
    group_rows = n // 2 * ROWS
    out = lax.broadcasted_iota(jnp.int32, (block_rows, per * group_rows), 0)
    src = lax.broadcasted_iota(jnp.int32, (block_rows, per * group_rows), 1)
    k, out = out // (block_rows // 2), lax.rem(out, block_rows // 2)
    unfold = jnp.where(src == lax.rem(out, per) * group_rows + out // per * ROWS + per + k, 1.0, 0.0).astype(bf16)

    def packed(gat, part):
        piece = gat[part * (n // 2):(part + 1) * (n // 2)]
        piece = piece.reshape(group_rows, gat.shape[2])
        folded = jnp.concatenate([piece[:, 128 * q:128 * (q + 1)] for q in range(per)], axis=0)
        tails = dot(unfold, folded, (1, 0))
        return jnp.concatenate([dot(dense, piece, (1, 0)), tails[:block_rows // 2], tails[block_rows // 2:]], axis=1)

    spread_a = Spread(rows_a, sem_b2.at[0], nz, z, at_z)
    spread_b = Spread(rows_b, sem_b2.at[1], ny, y, at_y)
    for part, group in ((0, near), (1, far)):
        for exchange, spread, gat in ((first_a, spread_a, gat_a), (first_b, spread_b, gat_b)):
            exchange.wait_recv(group)
            blocks = spread.blocks
            blocks[n // 2 - 1, part] = packed(gat, part).reshape(blocks.shape[2:]).astype(bf16)
            spread.start(part)
    for part in (0, 1):
        for spread in (spread_a, spread_b):
            spread.forward(part)
    for part in (0, 1):
        for spread in (spread_a, spread_b):
            spread.finish(part)

    def block_of(i):
        return (i - 1 + n // 2 - 1) % n

    all_a = rows_a[...].reshape(n * block_rows, lanes_a)
    all_b = rows_b[...].reshape(n * block_rows, lanes_b)
    for hid, rows, weights in ((hid_a, all_a, wa), (hid_b, all_b, wb)):
        product = dot(rows, weights[...], (1, 1))
        for i in range(n):
            here = product[block_of(i) * block_rows:(block_of(i) + 1) * block_rows]
            hid[0, i * block_rows:(i + 1) * block_rows] = here[:, :128]
            hid[1, i * block_rows:(i + 1) * block_rows] = here[:, 128:]

    def gathered(which, q):
        return jnp.concatenate([
            hid_a[which, pl.ds(i * block_rows + q, n, stride=per), :]
            + hid_b[which, pl.ds(i * per + q, n, stride=block_rows), :] for i in range(n)], axis=0)

    for c in range(CAP):
        pre_act = gathered(0, c)
        back_grad = gathered(1, CAP + c)
        gates = pre_act[:, hidden:hidden + 1]
        value, slope = gelu_parts(pre_act)
        used[0, c * n * n:(c + 1) * n * n] = gates * back_grad * slope
        used[1, c * n * n:(c + 1) * n * n] = gates * value

    full = half // 128

    def terms(rows, weights, send):
        result = dot(rows[:, :hidden].astype(bf16), weights, (1, 0))
        result = result.reshape(n, CAP, n, half)
        for c in range(CAP):
            for t in range(full):
                send[:, c * full + t] = result[:, c, :, 128 * t:128 * (t + 1)].astype(bf16)
        tails = [result[:, c, :, 128 * full:] for c in range(CAP)]
        tails.append(jnp.zeros((n, n, 128 - CAP * (half - 128 * full)), f32))
        send[:, CAP * full] = jnp.concatenate(tails, axis=2).astype(bf16)

    def first_sum(send, recv, sems, me, device_of):
        return Exchange(lambda d: send.at[place(d)], lambda d: recv.at[d], lambda d: recv.at[d], sems, n, me, device_of)

    order_a = [used[0, (c * n + i) * n:(c * n + i + 1) * n, :] for i in range(n) for c in range(CAP)]
    terms(jnp.concatenate(order_a, axis=0), w1[:, :half], send_da)
    sum_a = first_sum(send_da, recv_da, sem_d1.at[0], z, at_z)
    sum_a.start(far_first(n))
    order_b = [used[0, pl.ds(c * n * n + i, n, stride=n), :] for i in range(n) for c in range(CAP)]
    terms(jnp.concatenate(order_b, axis=0), w1b[...], send_db)
    sum_b = first_sum(send_db, recv_db, sem_d1.at[1], y, at_y)
    sum_b.start(far_first(n))

    for c in range(CAP):
        for i in range(n):
            for which in (0, 1):
                q = which * CAP + c
                piece = used[which, (c * n + i) * n:(c * n + i + 1) * n, :]
                used_a[which, pl.ds(block_of(i) * block_rows + q, n, stride=per), :] = piece
    for c in range(CAP):
        for i in range(n):
            for which in (0, 1):
                q = which * CAP + c
                piece = used[which, pl.ds(c * n * n + i, n, stride=n), :]
                used_b[which, pl.ds(block_of(i) * block_rows + q, n, stride=per), :] = piece

    for pieces, rows, first_lane, width in ((used_a, all_a, 0, lanes_a), (used_b, all_b, lanes_a, rest)):
        both = jnp.concatenate([pieces[0], pieces[1]], axis=1).astype(bf16)
        product = dot(both, rows, (0, 0))
        grad1[:, first_lane:first_lane + width] = product[:hidden, :width]
        grad2[:, first_lane:first_lane + width] = product[128:128 + hidden, :width]

    quarter = half // 2
    tiles = quarter // 128
    tail = quarter - 128 * tiles
    half_tail = half - 128 * full

    def second(exchange, send_first, recv, send, again, sems, me, device_of):
        exchange.wait_recv(far_first(n)[::-1])
        total = send_first[place(0)].astype(f32)
        for d in range(1, n):
            total = total + recv[d].astype(f32)
        tails = []
        for c in range(CAP):
            whole = [total[c * full + t] for t in range(full)]
            whole.append(total[CAP * full][:, c * half_tail:(c + 1) * half_tail])
            whole = jnp.concatenate(whole, axis=1)
            for h in (0, 1):
                for t in range(tiles):
                    start = h * quarter + 128 * t
                    send[t, pl.ds(h * CAP + c, n, stride=ROWS), :] = whole[:, start:start + 128]
                tails.append((h * CAP + c, whole[:, h * quarter + 128 * tiles:(h + 1) * quarter]))
        tails = [piece for _, piece in sorted(tails, key=lambda item: item[0])]
        tails.append(jnp.zeros((n, 128 - per * tail), f32))
        send[0, pl.ds(per, n, stride=ROWS), :] = jnp.concatenate(tails, axis=1)
        again_sum = Exchange(lambda d: send.at[:, pl.ds(place(d) * ROWS, ROWS)], lambda d: again.at[d], lambda d: again.at[d], sems, n, me, device_of)
        again_sum.start(far_first(n))
        return again_sum

    again_a = second(sum_a, send_da, recv_da, send_2a, recv_2a, sem_d2.at[0], y, at_y)
    again_b = second(sum_b, send_db, recv_db, send_2b, recv_2b, sem_d2.at[1], z, at_z)

    quarter_chunks = ne // 4
    for which, exchange, send, again in ((0, again_a, send_2a, recv_2a), (1, again_b, send_2b, recv_2b)):
        exchange.wait_recv(far_first(n)[::-1])
        total = send[:, place(0) * ROWS:(place(0) + 1) * ROWS]
        for d in range(1, n):
            total = total + again[d]
        tails = [total[0][per:per + 1, q * tail:(q + 1) * tail] for q in range(per)]
        tails.append(jnp.zeros((ROWS - per, tail), f32))
        total = jnp.concatenate([total[t] for t in range(tiles)] + [jnp.concatenate(tails, axis=0)], axis=1)
        for i in range(quarter_chunks):
            send_e[which * quarter_chunks + i] = total[:, i * chunk:(i + 1) * chunk].astype(bf16)

    def block_for(i):
        return i // (ne // 2) * quarter_chunks + lax.rem(i, quarter_chunks)

    back = Exchange(
        lambda d: send_e.at[block_for(lax.rem(e + d, ne))], lambda d: recv_e.at[e], lambda d: recv_e.at[lax.rem(e + ne - d, ne)],
        sem_e, ne, e, at_e)
    back.start(far_first(ne))
    recv_e[e] = send_e[block_for(e)]
    my_quarter = lax.rem(e, ne // 2) // quarter_chunks
    pick_e = jnp.where(row == key + my_quarter * CAP, 1.0, 0.0).astype(bf16)
    for exchange in (dispatch, first_a, first_b, spread_a, spread_b, sum_a, sum_b, again_a, again_b):
        exchange.wait_send()
    back.wait_recv(range(1, ne))
    branch = dot(pick_e, recv_e[...].reshape(ne * ROWS, chunk), (0, 0))
    tok_out[...] = (og[...].astype(f32) + branch).astype(bf16)
    back.wait_send()


def local(nz, ny, tokens, out_grad, gate_probs, expert_ids, slots, w_in, w_out):
    ne = lax.axis_size("expert")
    n = nz
    tokens_here, chunk = tokens.shape
    features = ne * chunk
    half = features // 2
    tiles = (features + 128) // 128
    lanes_a = 128 * ((tiles + 1) // 2)
    lanes_b = 128 * tiles - lanes_a
    w1 = jnp.swapaxes(w_in[0], 0, 1)
    w2 = w_out[0]
    hidden = w1.shape[0]
    cfg = (ne, nz, ny, chunk, lanes_a, lanes_b)
    vmem = pltpu.VMEM
    dma = pltpu.SemaphoreType.DMA
    per = 2 * CAP
    part_rows = n * per // 2
    step_rows = math.gcd(8, part_rows)
    scratch = [
        vmem((tokens_here, chunk), bf16),
        vmem((tokens_here, chunk), bf16),
        vmem((1, tokens_here), bf16),
        vmem((1, tokens_here), jnp.int32),
        vmem((1, tokens_here), jnp.int32),
        vmem((hidden, features), bf16),
        vmem((hidden, features), bf16),
        vmem((256, lanes_a), bf16),
        vmem((256, lanes_b), bf16),
        vmem((hidden, half), bf16),
        vmem((ne, ROWS, chunk), bf16),
        vmem((ne, ROWS, chunk), bf16),
        vmem((ROWS, lanes_a + lanes_b), f32),
        vmem((n, ROWS, lanes_a - 128 * (ROWS - per)), bf16),
        vmem((n, ROWS, lanes_b - 128 * (ROWS - per)), bf16),
        vmem((n, 2, part_rows // step_rows, step_rows, lanes_a), bf16),
        vmem((n, 2, part_rows // step_rows, step_rows, lanes_b), bf16),
        vmem((2, n * n * per, 128), f32),
        vmem((2, n * n * per, 128), f32),
        vmem((2, CAP * n * n, 128), f32),
        vmem((2, n * n * per, 128), f32),
        vmem((2, n * n * per, 128), f32),
        vmem((n, CAP * (half // 128) + 1, n, 128), bf16),
        vmem((n, CAP * (half // 128) + 1, n, 128), bf16),
        vmem((n, CAP * (half // 128) + 1, n, 128), bf16),
        vmem((n, CAP * (half // 128) + 1, n, 128), bf16),
        vmem((half // 2 // 128, n * ROWS, 128), f32),
        vmem((half // 2 // 128, n * ROWS, 128), f32),
        vmem((n, half // 2 // 128, ROWS, 128), f32),
        vmem((n, half // 2 // 128, ROWS, 128), f32),
        vmem((ne // 2, ROWS, chunk), bf16),
        vmem((ne, ROWS, chunk), bf16),
        dma((7,)),
        dma((2, ne)),
        dma((2, 2, n)),
        dma((2, 2, 8, 2)),
        dma((2, 2, n)),
        dma((2, 2, n)),
        dma((2, ne)),
    ]
    in_vmem = pl.BlockSpec(memory_space=pltpu.VMEM)
    in_hbm = pl.BlockSpec(memory_space=pltpu.HBM)
    operands = (tokens, out_grad, gate_probs[None], expert_ids[None], slots[None], w1, w2)
    token_grad, g1, g2 = pl.pallas_call(
        functools.partial(kernel, cfg),
        out_shape=(
            jax.ShapeDtypeStruct((tokens_here, chunk), bf16),
            jax.ShapeDtypeStruct((hidden, features), f32),
            jax.ShapeDtypeStruct((hidden, features), f32),
        ),
        in_specs=[in_hbm] * 7,
        out_specs=(in_vmem,) * 3,
        scratch_shapes=scratch,
        compiler_params=pltpu.CompilerParams(
            collective_id=0, has_side_effects=True, vmem_limit_bytes=48 * 1024 * 1024
        ),
        name="moe_backward",
    )(*[pltpu.with_memory_space_constraint(value, pltpu.HBM) for value in operands])
    return token_grad, jnp.swapaxes(g1, 0, 1)[None], g2[None]


def solution(mesh):
    placed = (
        P("shard", "expert"),
        P("shard", "expert"),
        P("shard"),
        P("shard"),
        P("shard"),
        P("expert", None, "shard"),
        P("expert", "shard", None),
    )
    ny = math.isqrt(mesh.shape["shard"])
    nz = mesh.shape["shard"] // ny
    return jax.shard_map(
        functools.partial(local, nz, ny),
        mesh=mesh,
        in_specs=placed,
        out_specs=(P("shard", "expert"), P("expert", None, "shard"), P("expert", "shard", None)),
        check_vma=False,
    )
```

```python
import functools
import math

import jax
import jax.numpy as jnp
from jax import lax
from jax.experimental import pallas as pl
from jax.experimental.pallas import tpu as pltpu
from jax.sharding import PartitionSpec as P

CAP = 3
ROWS = 8
MESH = pl.DeviceIdType.MESH
f32 = jnp.float32
bf16 = jnp.bfloat16

root_two_over_pi = 0.7978845608028654
cubic_coef = 0.044715


def gelu_parts(pre_act):
    inner = root_two_over_pi * (pre_act + cubic_coef * pre_act * pre_act * pre_act)
    tanh_val = jnp.tanh(inner)
    value = 0.5 * pre_act * (1.0 + tanh_val)
    slope = 0.5 * (1.0 + tanh_val) + 0.5 * pre_act * (
        1.0 - tanh_val * tanh_val
    ) * root_two_over_pi * (1.0 + 3.0 * cubic_coef * pre_act * pre_act)
    return value, slope


def dot(left, right, contract):
    return lax.dot_general(left, right, ((contract[:1], contract[1:]), ((), ())), preferred_element_type=f32)


def remote(src, dst, send_sem, recv_sem, device):
    return pltpu.make_async_remote_copy(
        src_ref=src, dst_ref=dst, send_sem=send_sem, recv_sem=recv_sem, device_id=device, device_id_type=MESH
    )


class Exchange:
    def __init__(self, src, dst, got, sems, n, me, device_of):
        self.src, self.dst, self.got, self.sems, self.n, self.me, self.device_of = src, dst, got, sems, n, me, device_of

    def copy(self, d):
        device = self.device_of(lax.rem(self.me + d, self.n))
        return remote(self.src(d), self.dst(d), self.sems.at[0, d], self.sems.at[1, d], device)

    def start(self, order):
        for d in order:
            self.copy(d).start()

    def wait_recv(self, order):
        for d in order:
            here = self.got(d)
            device = self.device_of(lax.rem(self.me + self.n - d, self.n))
            remote(here, here, self.sems.at[0, d], self.sems.at[1, d], device).wait_recv()

    def wait_send(self):
        for d in range(1, self.n):
            self.copy(d).wait_send()


def far_first(n):
    return sorted(range(1, n), key=lambda d: -min(d, n - d))


class Spread:
    def __init__(self, blocks, sems, n, me, device_of):
        self.blocks, self.sems, self.n, self.me, self.device_of = blocks, sems, n, me, device_of
        self.waited = set()
        self.sent = []
        if n > 4:
            self.first = {0: (-2, 2), 1: (2, -2), 2: (-1, 1), 3: (1, -1)}
            self.second = {4: (-3, 1), 5: (3, -1), 6: (4, 1), 7: (4, -2)}
        else:
            self.first = {0: (1, 1)}
            self.second = {}

    def block(self, distance, part):
        return self.blocks.at[(distance + self.n // 2 - 1) % self.n, part]

    def copy(self, index, part):
        distance, places = {**self.first, **self.second}[index]
        device = self.device_of(lax.rem(self.me + places + self.n, self.n))
        src, dst = self.block(distance + places, part), self.block(distance, part)
        return remote(src, dst, self.sems.at[0, index, part], self.sems.at[1, index, part], device)

    def send(self, index, part):
        copy = self.copy(index, part)
        copy.start()
        self.sent.append(copy)

    def receive(self, index, part):
        if (index, part) in self.waited:
            return
        self.waited.add((index, part))
        distance, places = {**self.first, **self.second}[index]
        device = self.device_of(lax.rem(self.me - places + self.n, self.n))
        here = self.block(distance, part)
        remote(here, here, self.sems.at[0, index, part], self.sems.at[1, index, part], device).wait_recv()

    def start(self, part):
        for index in self.first:
            self.send(index, part)

    def forward(self, part):
        if self.second:
            for index, through, across in ((0, 4, 6), (1, 5, 7)):
                self.receive(index, part)
                if part == index == 1:
                    self.send(across, part)
                self.send(through, part)

    def third(self):
        if self.second:
            self.receive(4, 0)
            self.send(6, 0)

    def finish_first(self, part):
        for index in self.first:
            self.receive(index, part)

    def finish(self, part):
        self.finish_first(part)
        if self.second:
            for index in (4, 5, 6 + part):
                self.receive(index, part)

    def wait_send(self):
        for copy in self.sent:
            copy.wait_send()


def kernel(
    cfg, tok_hbm, og_hbm, gate_hbm, ids_hbm, slots_hbm, w1_hbm, w2_hbm,
    tok_out, grad1, grad2,
    tok, og, gate, ids, slots, w1, w2, wa, wb, w1b,
    send_a, recv_a, flat, gat_a, gat_b, rows_a, rows_b, hid_a, hid_b, used, used_a, used_b,
    send_da, send_db, recv_da, recv_db, send_2a, send_2b, recv_2a, recv_2b,
    send_e, recv_e,
    sem_w, sem_a, sem_b1, sem_b2, sem_d1, sem_d2, sem_e,
):
    ne, nz, ny, chunk, lanes_a, lanes_b = cfg
    n = nz
    features = ne * chunk
    half = features // 2
    rest = features - lanes_a
    hidden = w1.shape[0]
    per = 2 * CAP
    block_rows = n * per
    count = CAP * n * n
    e = lax.axis_index("expert")
    s = lax.axis_index("shard")
    z, y = s // ny, lax.rem(s, ny)

    def at_e(i):
        return (i, s)

    def at_z(i):
        return (e, i * ny + y)

    def at_y(i):
        return (e, z * ny + i)

    sources = (tok_hbm, og_hbm, gate_hbm, ids_hbm, slots_hbm, w1_hbm, w2_hbm)
    places = (tok, og, gate, ids, slots, w1, w2)
    loads = [pltpu.make_async_copy(src, dst, sem_w.at[i]) for i, (src, dst) in enumerate(zip(sources, places))]
    for load in loads:
        load.start()

    barrier = pltpu.get_barrier_semaphore()
    for device_of, me, size in ((at_e, e, ne), (at_z, z, nz), (at_y, y, ny)):
        for d in far_first(size):
            pl.semaphore_signal(barrier, inc=1, device_id=device_of(lax.rem(me + d, size)), device_id_type=MESH)

    for load in loads[:5]:
        load.wait()
    key = jnp.where(slots[...] >= 0, ids[...] * ROWS + slots[...], -100)
    row = lax.broadcasted_iota(jnp.int32, (ne * ROWS, tok.shape[0]), 0)
    pick_x = jnp.where(row == key, 1.0, 0.0).astype(bf16)
    pick_g = jnp.where(row == key + CAP, 1.0, 0.0).astype(bf16)
    sent = dot(pick_x, tok[...], (1, 0)) + dot(pick_g, og[...], (1, 0))
    send_a[...] = sent.reshape(ne, ROWS, chunk).astype(bf16)
    row8 = lax.broadcasted_iota(jnp.int32, (ROWS, tok.shape[0]), 0) + e * ROWS
    gate_rows = jnp.sum(jnp.where(row8 == key, gate[...].astype(f32), 0.0), axis=1, keepdims=True)
    flat[:, features - features % 128:] = jnp.zeros((ROWS, flat.shape[1] - features + features % 128), f32)
    flat[:, features:features + 1] = gate_rows

    pl.semaphore_wait(barrier, (ne - 1) + (nz - 1) + (ny - 1))

    dispatch = Exchange(
        lambda d: send_a.at[lax.rem(e + d, ne)], lambda d: recv_a.at[e], lambda d: recv_a.at[lax.rem(e + ne - d, ne)],
        sem_a, ne, e, at_e)
    dispatch.start(far_first(ne))
    recv_a[e] = send_a[e]

    loads[5].wait()
    loads[6].wait()
    wa[...] = jnp.zeros(wa.shape, bf16)
    wb[...] = jnp.zeros(wb.shape, bf16)
    wa[:hidden] = w1[:, :lanes_a]
    wa[128:128 + hidden] = w2[:, :lanes_a]
    wb[:hidden, :rest] = w1[:, lanes_a:]
    wb[128:128 + hidden, :rest] = w2[:, lanes_a:]
    gate_unit = lax.broadcasted_iota(jnp.int32, (16, lanes_b), 0) == 0
    gate_lane = lax.broadcasted_iota(jnp.int32, (16, lanes_b), 1) == rest
    wb[hidden:hidden + 16] = jnp.where(jnp.logical_and(gate_unit, gate_lane), 1.0, 0.0).astype(bf16)
    w1b[...] = w1[:, half:]
    used_a[...] = jnp.zeros(used_a.shape, f32)
    used_b[...] = jnp.zeros(used_b.shape, f32)
    send_2a[...] = jnp.zeros(send_2a.shape, f32)
    send_2b[...] = jnp.zeros(send_2b.shape, f32)

    dispatch.wait_recv(range(1, ne))
    for i in range(ne):
        flat[:, i * chunk:(i + 1) * chunk] = recv_a[i].astype(f32)
    for base, gat in ((0, gat_a), (lanes_a, gat_b)):
        for k in range(ROWS - per):
            tail = base + gat.shape[2] + 128 * k
            for q in range(per):
                flat[per + k:per + k + 1, base + 128 * q:base + 128 * (q + 1)] = flat[q:q + 1, tail:tail + 128]

    def place(distance):
        return (distance + 1) % n

    def first(gat, sems, me, device_of):
        mine = place(0)
        return Exchange(lambda d: gat.at[mine], lambda d: gat.at[place(-d)], lambda d: gat.at[place(-d)], sems, n, me, device_of)

    near = [d for d in range(1, n) if place(-d) < n // 2]
    far = [d for d in range(1, n) if place(-d) >= n // 2]
    first_a = first(gat_a, sem_b1.at[0], y, at_y)
    first_b = first(gat_b, sem_b1.at[1], z, at_z)
    gat_a[place(0)] = flat[:, :gat_a.shape[2]].astype(bf16)
    first_a.start(near + far)
    gat_b[place(0)] = flat[:, lanes_a:lanes_a + gat_b.shape[2]].astype(bf16)
    first_b.start(near + far)

    out = lax.broadcasted_iota(jnp.int32, (block_rows // 2, n // 2 * ROWS), 0)
    src = lax.broadcasted_iota(jnp.int32, (block_rows // 2, n // 2 * ROWS), 1)
    dense = jnp.where(src == out // per * ROWS + lax.rem(out, per), 1.0, 0.0).astype(bf16)
    group_rows = n // 2 * ROWS
    out = lax.broadcasted_iota(jnp.int32, (block_rows, per * group_rows), 0)
    src = lax.broadcasted_iota(jnp.int32, (block_rows, per * group_rows), 1)
    k, out = out // (block_rows // 2), lax.rem(out, block_rows // 2)
    unfold = jnp.where(src == lax.rem(out, per) * group_rows + out // per * ROWS + per + k, 1.0, 0.0).astype(bf16)

    def packed(gat, part):
        piece = gat[part * (n // 2):(part + 1) * (n // 2)]
        piece = piece.reshape(group_rows, gat.shape[2])
        folded = jnp.concatenate([piece[:, 128 * q:128 * (q + 1)] for q in range(per)], axis=0)
        tails = dot(unfold, folded, (1, 0))
        return jnp.concatenate([dot(dense, piece, (1, 0)), tails[:block_rows // 2], tails[block_rows // 2:]], axis=1)

    spread_a = Spread(rows_a, sem_b2.at[0], nz, z, at_z)
    spread_b = Spread(rows_b, sem_b2.at[1], ny, y, at_y)
    for part, group in ((0, near), (1, far)):
        for exchange, spread, gat in ((first_a, spread_a, gat_a), (first_b, spread_b, gat_b)):
            exchange.wait_recv(group)
            blocks = spread.blocks
            blocks[n // 2 - 1, part] = packed(gat, part).reshape(blocks.shape[2:]).astype(bf16)
            spread.start(part)
    for part in (0, 1):
        for spread in (spread_a, spread_b):
            spread.forward(part)
    for spread in (spread_a, spread_b):
        spread.third()
    def block_of(i):
        return (i - 1 + n // 2 - 1) % n

    early = [i for i in range(n) if n > 4 and 1 <= block_of(i) <= n - 3]
    late = [i for i in range(n) if i not in early]

    def products(places, count):
        for hid, rows, weights in ((hid_a, rows_a, wa), (hid_b, rows_b, wb)):
            width = rows.shape[-1]
            if count:
                block = rows[1:1 + count]
            else:
                block = jnp.concatenate([rows[block_of(i):block_of(i) + 1] for i in places], axis=0)
            product = dot(block.reshape(len(places) * block_rows, width), weights[...], (1, 1))
            for k, i in enumerate(sorted(places, key=block_of) if count else places):
                here = product[k * block_rows:(k + 1) * block_rows]
                hid[0, i * block_rows:(i + 1) * block_rows] = here[:, :128]
                hid[1, i * block_rows:(i + 1) * block_rows] = here[:, 128:]

    if early:
        for part in (0, 1):
            for spread in (spread_a, spread_b):
                spread.finish_first(part)
        products(early, len(early))
    for part in (0, 1):
        for spread in (spread_a, spread_b):
            spread.finish(part)
    products(late, 0)
    all_a = rows_a[...].reshape(n * block_rows, lanes_a)
    all_b = rows_b[...].reshape(n * block_rows, lanes_b)

    def gathered(which, q):
        return jnp.concatenate([
            hid_a[which, pl.ds(i * block_rows + q, n, stride=per), :]
            + hid_b[which, pl.ds(i * per + q, n, stride=block_rows), :] for i in range(n)], axis=0)

    for c in range(CAP):
        pre_act = gathered(0, c)
        back_grad = gathered(1, CAP + c)
        gates = pre_act[:, hidden:hidden + 1]
        value, slope = gelu_parts(pre_act)
        used[0, c * n * n:(c + 1) * n * n] = gates * back_grad * slope
        used[1, c * n * n:(c + 1) * n * n] = gates * value

    full = half // 128

    def terms(rows, weights, send):
        result = dot(rows[:, :hidden].astype(bf16), weights, (1, 0))
        result = result.reshape(n, CAP, n, half)
        for c in range(CAP):
            for t in range(full):
                send[:, c * full + t] = result[:, c, :, 128 * t:128 * (t + 1)].astype(bf16)
        tails = [result[:, c, :, 128 * full:] for c in range(CAP)]
        tails.append(jnp.zeros((n, n, 128 - CAP * (half - 128 * full)), f32))
        send[:, CAP * full] = jnp.concatenate(tails, axis=2).astype(bf16)

    def first_sum(send, recv, sems, me, device_of):
        return Exchange(lambda d: send.at[place(d)], lambda d: recv.at[d], lambda d: recv.at[d], sems, n, me, device_of)

    order_a = [used[0, (c * n + i) * n:(c * n + i + 1) * n, :] for i in range(n) for c in range(CAP)]
    terms(jnp.concatenate(order_a, axis=0), w1[:, :half], send_da)
    sum_a = first_sum(send_da, recv_da, sem_d1.at[0], z, at_z)
    sum_a.start(far_first(n))
    order_b = [used[0, pl.ds(c * n * n + i, n, stride=n), :] for i in range(n) for c in range(CAP)]
    terms(jnp.concatenate(order_b, axis=0), w1b[...], send_db)
    sum_b = first_sum(send_db, recv_db, sem_d1.at[1], y, at_y)
    sum_b.start(far_first(n))

    for c in range(CAP):
        for i in range(n):
            for which in (0, 1):
                q = which * CAP + c
                piece = used[which, (c * n + i) * n:(c * n + i + 1) * n, :]
                used_a[which, pl.ds(block_of(i) * block_rows + q, n, stride=per), :] = piece
    for c in range(CAP):
        for i in range(n):
            for which in (0, 1):
                q = which * CAP + c
                piece = used[which, pl.ds(c * n * n + i, n, stride=n), :]
                used_b[which, pl.ds(block_of(i) * block_rows + q, n, stride=per), :] = piece

    for pieces, rows, first_lane, width in ((used_a, all_a, 0, lanes_a), (used_b, all_b, lanes_a, rest)):
        both = jnp.concatenate([pieces[0], pieces[1]], axis=1).astype(bf16)
        product = dot(both, rows, (0, 0))
        grad1[:, first_lane:first_lane + width] = product[:hidden, :width]
        grad2[:, first_lane:first_lane + width] = product[128:128 + hidden, :width]

    quarter = half // 2
    tiles = quarter // 128
    tail = quarter - 128 * tiles
    half_tail = half - 128 * full

    def second(exchange, send_first, recv, send, again, sems, me, device_of):
        exchange.wait_recv(far_first(n)[::-1])
        total = send_first[place(0)].astype(f32)
        for d in range(1, n):
            total = total + recv[d].astype(f32)
        tails = []
        for c in range(CAP):
            whole = [total[c * full + t] for t in range(full)]
            whole.append(total[CAP * full][:, c * half_tail:(c + 1) * half_tail])
            whole = jnp.concatenate(whole, axis=1)
            for h in (0, 1):
                for t in range(tiles):
                    start = h * quarter + 128 * t
                    send[t, pl.ds(h * CAP + c, n, stride=ROWS), :] = whole[:, start:start + 128]
                tails.append((h * CAP + c, whole[:, h * quarter + 128 * tiles:(h + 1) * quarter]))
        tails = [piece for _, piece in sorted(tails, key=lambda item: item[0])]
        tails.append(jnp.zeros((n, 128 - per * tail), f32))
        send[0, pl.ds(per, n, stride=ROWS), :] = jnp.concatenate(tails, axis=1)
        again_sum = Exchange(lambda d: send.at[:, pl.ds(place(d) * ROWS, ROWS)], lambda d: again.at[d], lambda d: again.at[d], sems, n, me, device_of)
        again_sum.start(far_first(n))
        return again_sum

    again_a = second(sum_a, send_da, recv_da, send_2a, recv_2a, sem_d2.at[0], y, at_y)
    again_b = second(sum_b, send_db, recv_db, send_2b, recv_2b, sem_d2.at[1], z, at_z)

    quarter_chunks = ne // 4
    for which, exchange, send, again in ((0, again_a, send_2a, recv_2a), (1, again_b, send_2b, recv_2b)):
        exchange.wait_recv(far_first(n)[::-1])
        total = send[:, place(0) * ROWS:(place(0) + 1) * ROWS]
        for d in range(1, n):
            total = total + again[d]
        tails = [total[0][per:per + 1, q * tail:(q + 1) * tail] for q in range(per)]
        tails.append(jnp.zeros((ROWS - per, tail), f32))
        total = jnp.concatenate([total[t] for t in range(tiles)] + [jnp.concatenate(tails, axis=0)], axis=1)
        for i in range(quarter_chunks):
            send_e[which * quarter_chunks + i] = total[:, i * chunk:(i + 1) * chunk].astype(bf16)

    def block_for(i):
        return i // (ne // 2) * quarter_chunks + lax.rem(i, quarter_chunks)

    back = Exchange(
        lambda d: send_e.at[block_for(lax.rem(e + d, ne))], lambda d: recv_e.at[e], lambda d: recv_e.at[lax.rem(e + ne - d, ne)],
        sem_e, ne, e, at_e)
    back.start(far_first(ne))
    recv_e[e] = send_e[block_for(e)]
    my_quarter = lax.rem(e, ne // 2) // quarter_chunks
    pick_e = jnp.where(row == key + my_quarter * CAP, 1.0, 0.0).astype(bf16)
    for exchange in (dispatch, first_a, first_b, spread_a, spread_b, sum_a, sum_b, again_a, again_b):
        exchange.wait_send()
    back.wait_recv(range(1, ne))
    branch = dot(pick_e, recv_e[...].reshape(ne * ROWS, chunk), (0, 0))
    tok_out[...] = (og[...].astype(f32) + branch).astype(bf16)
    back.wait_send()


def local(nz, ny, tokens, out_grad, gate_probs, expert_ids, slots, w_in, w_out):
    ne = lax.axis_size("expert")
    n = nz
    tokens_here, chunk = tokens.shape
    features = ne * chunk
    half = features // 2
    tiles = (features + 128) // 128
    lanes_a = 128 * ((tiles + 1) // 2)
    lanes_b = 128 * tiles - lanes_a
    w1 = jnp.swapaxes(w_in[0], 0, 1)
    w2 = w_out[0]
    hidden = w1.shape[0]
    cfg = (ne, nz, ny, chunk, lanes_a, lanes_b)
    vmem = pltpu.VMEM
    dma = pltpu.SemaphoreType.DMA
    per = 2 * CAP
    part_rows = n * per // 2
    step_rows = math.gcd(8, part_rows)
    scratch = [
        vmem((tokens_here, chunk), bf16),
        vmem((tokens_here, chunk), bf16),
        vmem((1, tokens_here), bf16),
        vmem((1, tokens_here), jnp.int32),
        vmem((1, tokens_here), jnp.int32),
        vmem((hidden, features), bf16),
        vmem((hidden, features), bf16),
        vmem((256, lanes_a), bf16),
        vmem((256, lanes_b), bf16),
        vmem((hidden, half), bf16),
        vmem((ne, ROWS, chunk), bf16),
        vmem((ne, ROWS, chunk), bf16),
        vmem((ROWS, lanes_a + lanes_b), f32),
        vmem((n, ROWS, lanes_a - 128 * (ROWS - per)), bf16),
        vmem((n, ROWS, lanes_b - 128 * (ROWS - per)), bf16),
        vmem((n, 2, part_rows // step_rows, step_rows, lanes_a), bf16),
        vmem((n, 2, part_rows // step_rows, step_rows, lanes_b), bf16),
        vmem((2, n * n * per, 128), f32),
        vmem((2, n * n * per, 128), f32),
        vmem((2, CAP * n * n, 128), f32),
        vmem((2, n * n * per, 128), f32),
        vmem((2, n * n * per, 128), f32),
        vmem((n, CAP * (half // 128) + 1, n, 128), bf16),
        vmem((n, CAP * (half // 128) + 1, n, 128), bf16),
        vmem((n, CAP * (half // 128) + 1, n, 128), bf16),
        vmem((n, CAP * (half // 128) + 1, n, 128), bf16),
        vmem((half // 2 // 128, n * ROWS, 128), f32),
        vmem((half // 2 // 128, n * ROWS, 128), f32),
        vmem((n, half // 2 // 128, ROWS, 128), f32),
        vmem((n, half // 2 // 128, ROWS, 128), f32),
        vmem((ne // 2, ROWS, chunk), bf16),
        vmem((ne, ROWS, chunk), bf16),
        dma((7,)),
        dma((2, ne)),
        dma((2, 2, n)),
        dma((2, 2, 8, 2)),
        dma((2, 2, n)),
        dma((2, 2, n)),
        dma((2, ne)),
    ]
    in_vmem = pl.BlockSpec(memory_space=pltpu.VMEM)
    in_hbm = pl.BlockSpec(memory_space=pltpu.HBM)
    operands = (tokens, out_grad, gate_probs[None], expert_ids[None], slots[None], w1, w2)
    token_grad, g1, g2 = pl.pallas_call(
        functools.partial(kernel, cfg),
        out_shape=(
            jax.ShapeDtypeStruct((tokens_here, chunk), bf16),
            jax.ShapeDtypeStruct((hidden, features), f32),
            jax.ShapeDtypeStruct((hidden, features), f32),
        ),
        in_specs=[in_hbm] * 7,
        out_specs=(in_vmem,) * 3,
        scratch_shapes=scratch,
        compiler_params=pltpu.CompilerParams(
            collective_id=0, has_side_effects=True, vmem_limit_bytes=48 * 1024 * 1024
        ),
        name="moe_backward",
    )(*[pltpu.with_memory_space_constraint(value, pltpu.HBM) for value in operands])
    return token_grad, jnp.swapaxes(g1, 0, 1)[None], g2[None]


def solution(mesh):
    placed = (
        P("shard", "expert"),
        P("shard", "expert"),
        P("shard"),
        P("shard"),
        P("shard"),
        P("expert", None, "shard"),
        P("expert", "shard", None),
    )
    ny = math.isqrt(mesh.shape["shard"])
    nz = mesh.shape["shard"] // ny
    return jax.shard_map(
        functools.partial(local, nz, ny),
        mesh=mesh,
        in_specs=placed,
        out_specs=(P("shard", "expert"), P("expert", None, "shard"), P("expert", "shard", None)),
        check_vma=False,
    )
```
